32 devices in a mesh: col: 4 (over x, core), gx: 4 (over z), gy: 2 (over y).
Axes of the slice: x: 2, y: 2, z: 4, core: 2. Of those that a mesh axis runs over, the one named last changes fastest.
Arguments:
- volume: float32 [32, 8, 16, 256], P('col', None, 'gx', 'gy'), may hold values from -6 to 6
- filters: float32 [32, 32, 3, 3, 3], P('col'), may hold values from -0.21875 to 0.21875
- upstream: float32 [32, 8, 16, 256], P('col', None, 'gx', 'gy'), may hold values from -6 to 6
Outputs:
- response: float32 [32, 8, 16, 256], P('col', None, 'gx', 'gy')
- input_grad: float32 [32, 8, 16, 256], P('col', None, 'gx', 'gy')
- filter_grad: float32 [32, 32, 3, 3, 3], P('col')
The draws below stay inside these ranges and needn't reach their ends.
All inputs are finite; a program needn't handle non-finite values.
Results may differ from the reference program's by a relative error of at most 0.0003.
Values sent between devices are 32-bit elements; how exact they have to be, the bound alone decides.
A program may use at most 64 MiB of HBM per device.

```python
import jax
import jax.numpy as jnp
from jax import lax

C_IN = 32
C_OUT = 32
PLANES = 8
NX = 16
NY = 256


def steps_of(rng, shape, pieces, smallest, top_value):
    loudness = 1.0
    for position, shards_of in pieces:
        heights = jax.random.uniform(jax.random.fold_in(jax.random.fold_in(rng, 6), position), (shards_of,), jnp.float32, smallest / len(pieces), top_value / len(pieces))
        loudness = loudness * jnp.repeat(jnp.exp(heights), shape[position] // shards_of).reshape((-1,) + (1,) * (len(shape) - 1 - position))
    return loudness


def scatter_about(key, shape, scale, reach, cuts=(), kind=jnp.bfloat16):
    values = scale * jax.random.normal(key, shape, jnp.float32)
    if cuts:
        values = values * steps_of(key, shape, cuts, -0.22, 0.18)
    return jnp.clip(values, -reach, reach).astype(kind)


def setup_inputs(seed: int = 0) -> dict:
    streams_of = jax.random.split(jax.random.key(seed), 4)
    return {
        "volume": scatter_about(streams_of[0], (C_IN, PLANES, NX, NY), 1.0, 6.0, ((0, 4), (2, 4), (3, 2)), jnp.float32),
        "filters": scatter_about(streams_of[1], (C_OUT, C_IN, 3, 3, 3), (C_IN * 27) ** -0.5, 0.21875, ((0, 4),), jnp.float32),
        "upstream": scatter_about(streams_of[2], (C_OUT, PLANES, NX, NY), 1.0, 6.0, ((0, 4), (2, 4), (3, 2)), jnp.float32),
    }


def convolve(volume, filters):
    result = lax.conv_general_dilated(volume[None], filters, (1, 1, 1), ((1, 1), (1, 1), (1, 1)), dimension_numbers=('NCDHW', 'OIDHW', 'NCDHW'), precision=lax.Precision.HIGHEST)
    return result[0]

def reference(volume, filters, upstream):
    response, backward = jax.vjp(convolve, volume, filters)
    input_grad, weight_total = backward(upstream)
    scale = (PLANES * NX * NY) ** (-0.5)
    return (response, input_grad, weight_total * scale)
```

```python
import functools

import jax
import jax.numpy as jnp
from jax import lax
from jax.experimental import pallas as pl
from jax.experimental.pallas import tpu as pltpu
from jax.sharding import PartitionSpec as P

MESH = pl.DeviceIdType.MESH
F32 = jnp.float32
BF16 = jnp.bfloat16
DIRS = [(-1, 0), (1, 0), (-1, -1), (0, -1), (1, -1), (-1, 1), (0, 1), (1, 1)]
TAPS = [(a, b, e) for a in range(3) for b in range(3) for e in range(3)]
PIECES = 7


def split(value):
    high = value.astype(BF16).astype(F32)
    return jnp.concatenate([high, value - high], axis=0).astype(BF16)


def kernel(
    nx, ny, planes, rows, scale,
    v_hbm, w_hbm, u_hbm,
    resp_ref, grad_ref, fg_ref,
    v_in, w_in, u_in, vx, x2, u_own, u_row, pack_out, pack_in, u3, igp, rs,
    acc, local, row_in, rpack_out, rpack_in, gpack, grecv, gfin,
    in_sem, v_send, v_recv, u_send, u_recv, g_send, g_recv, r_send, r_recv,
    s1_send, s1_recv, s2_send, s2_recv,
):
    col, gx, gy = lax.axis_index("col"), lax.axis_index("gx"), lax.axis_index("gy")
    group = nx * ny
    me = gx * ny + gy
    cells = planes * rows
    low, high = col % 2, col // 2
    core = high * 2 + (1 - low)
    chip = (1 - high) * 2 + low
    far = (1 - high) * 2 + (1 - low)

    def exists(dx, dy):
        ok = None
        for d, at, size in ((dx, gx, nx), (dy, gy, ny)):
            if d:
                term = (at + d >= 0) & (at + d < size)
                ok = term if ok is None else ok & term
        return ok

    loads = [
        pltpu.make_async_copy(s, d, in_sem.at[i])
        for i, (s, d) in enumerate(((v_hbm, v_in), (u_hbm, u_in), (w_hbm, w_in)))
    ]
    for load in loads:
        load.start()
    barrier = pltpu.get_barrier_semaphore()

    u_row[...] = jnp.zeros_like(u_row)
    pack_in[...] = jnp.zeros_like(pack_in)
    row_in[...] = jnp.zeros_like(row_in)
    rpack_in[...] = jnp.zeros_like(rpack_in)

    for other in (core, chip):
        pl.semaphore_signal(barrier, inc=1, device_id={"col": other}, device_id_type=MESH)

    def greet(j, carry):
        @pl.when(j != me)
        def _():
            pl.semaphore_signal(
                barrier, inc=1, device_id={"gx": j // ny, "gy": j % ny}, device_id_type=MESH
            )
        return carry

    lax.fori_loop(0, group, greet, 0)

    lane = lax.broadcasted_iota(jnp.int32, (8, 128), 1)
    loads[0].wait()
    for i in range(cells):
        vx[col, i] = v_in[pl.ds(i, 8, stride=cells), :]
    loads[1].wait()
    for i in range(cells):
        u_own[i // rows, i % rows] = u_in[pl.ds(i, 8, stride=cells), :]
    pack = jnp.zeros((8, 128), F32)
    for z in range(planes):
        for x in range(rows):
            at = z * 8 + x + 1
            tile = u_own[z, x]
            pack = jnp.where(lane == at, pltpu.roll(tile, at + 1, 1), pack)
            pack = jnp.where(lane == at + 64, pltpu.roll(tile, at + 64, 1), pack)
    pack_out[...] = pack

    pl.semaphore_wait(barrier, group + 1)

    def v_copy(slot, sem, target):
        return pltpu.make_async_remote_copy(
            src_ref=vx.at[slot], dst_ref=vx.at[slot], send_sem=v_send.at[sem],
            recv_sem=v_recv.at[sem], device_id={"col": target}, device_id_type=MESH,
        )

    def u_copy(d):
        dx, dy = DIRS[d]
        if dy == 0:
            src = u_own.at[:, 0 if dx < 0 else rows - 1]
            dst = u_row.at[d]
        else:
            src, dst = pack_out, pack_in.at[d - 2]
        return pltpu.make_async_remote_copy(
            src_ref=src, dst_ref=dst, send_sem=u_send.at[d], recv_sem=u_recv.at[d],
            device_id={"gx": gx + dx, "gy": gy + dy}, device_id_type=MESH,
        )

    def r_copy(d):
        dx, dy = DIRS[d]
        if dy == 0:
            src, dst = local.at[0 if dx < 0 else rows + 1], row_in.at[d]
        else:
            src, dst = rpack_out, rpack_in.at[d - 2]
        return pltpu.make_async_remote_copy(
            src_ref=src, dst_ref=dst, send_sem=r_send.at[d], recv_sem=r_recv.at[d],
            device_id={"gx": gx + dx, "gy": gy + dy}, device_id_type=MESH,
        )

    def each(copies, what, sender):
        for d, (dx, dy) in enumerate(DIRS):
            @pl.when(exists(dx, dy) if sender else exists(-dx, -dy))
            def _():
                getattr(copies(d), what)()

    each(u_copy, "start", True)
    v_chip, v_core = v_copy(col, 0, chip), v_copy(col, 1, core)
    v_chip.start()
    v_core.start()

    loads[2].wait()
    w = w_in[...]
    taps8 = w.shape[0]
    w_hi = w.astype(BF16)
    w_lo = (w - w_hi.astype(F32)).astype(BF16)
    c_at = lax.broadcasted_iota(jnp.int32, (32, 128), 0)
    k_at = lax.broadcasted_iota(jnp.int32, (32, 128), 1)
    same = ((k_at % 64) // 16 == c_at // 8) & (k_at % 8 == c_at % 8)
    pick_hi = jnp.where(same & (k_at < 64), 1.0, 0.0).astype(BF16)
    pick_lo = jnp.where(same & (k_at >= 64), 1.0, 0.0).astype(BF16)
    w_fwd = (
        jnp.dot(w_hi, pick_hi, preferred_element_type=F32)
        + jnp.dot(w_lo, pick_lo, preferred_element_type=F32)
    ).astype(BF16)
    eye_r = lax.broadcasted_iota(jnp.int32, (32, 32), 0)
    eye_c = lax.broadcasted_iota(jnp.int32, (32, 32), 1)
    eye = jnp.where(eye_r == eye_c, 1.0, 0.0).astype(BF16)
    d_r = lax.broadcasted_iota(jnp.int32, (taps8, 2 * taps8), 0)
    d_c = lax.broadcasted_iota(jnp.int32, (taps8, 2 * taps8), 1)
    twice = jnp.where((d_r // 8 == d_c // 16) & (d_r % 8 == d_c % 8), 1.0, 0.0).astype(BF16)
    nt = (((1,), (1,)), ((), ()))
    w_back = []
    for part in (w_hi, w_lo):
        turned = lax.dot_general(eye, part, nt, preferred_element_type=F32).astype(BF16)
        w_back.append(jnp.dot(turned, twice, preferred_element_type=F32))
    w_back = jnp.concatenate(w_back, axis=0).astype(BF16)

    each(u_copy, "wait_recv", False)
    spot = lane % 8
    edge = jnp.zeros((8, 128), F32)
    for first, keep in ((3, lane < 64), (0, lane >= 64)):
        before, mid, after = pack_in[first + 2], pack_in[first + 1], pack_in[first]
        total = jnp.where((spot >= 1) & (spot <= rows), mid, 0.0)
        total = jnp.where(spot == 0, pltpu.roll(before, 128 - rows, 1), total)
        total = jnp.where(spot == rows + 1, pltpu.roll(after, rows, 1), total)
        edge = jnp.where(keep, total, edge)
    zero16 = jnp.zeros((16, 128), BF16)
    for e in range(3):
        for x in range(rows + 2):
            u3[e, 0, x] = zero16
            u3[e, planes + 1, x] = zero16
    for z in range(planes):
        for x in range(rows + 2):
            at = z * 8 + x
            if x == 0:
                tile = u_row[1, z]
            elif x == rows + 1:
                tile = u_row[0, z]
            else:
                tile = u_own[z, x - 1]
            left = jnp.where(
                lane == 127, pltpu.roll(edge, (127 - 64 - at) % 128, 1), pltpu.roll(tile, 127, 1)
            )
            right = jnp.where(
                lane == 0, pltpu.roll(edge, (128 - at) % 128, 1), pltpu.roll(tile, 1, 1)
            )
            u3[0, z + 1, x] = split(left)
            u3[1, z + 1, x] = split(tile)
            u3[2, z + 1, x] = split(right)

    def stack(z):
        return jnp.concatenate(
            [
                jnp.concatenate([u3[e, z + 2 - a, x + 2 - b] for a, b, e in TAPS], axis=0)
                for x in range(rows)
            ],
            axis=1,
        )

    def back(z, carry):
        both = jnp.dot(w_back, stack(z), preferred_element_type=F32)
        for g in range(4):
            for x in range(rows):
                lanes = slice(x * 128, (x + 1) * 128)
                igp[g, z * rows + x] = (
                    both[g * 8 : g * 8 + 8, lanes] + both[32 + g * 8 : 40 + g * 8, lanes]
                )
        return carry

    lax.fori_loop(0, planes, back, 0)

    def g_copy(slot, to, target):
        return pltpu.make_async_remote_copy(
            src_ref=igp.at[slot], dst_ref=rs.at[to], send_sem=g_send.at[to],
            recv_sem=g_recv.at[to], device_id={"col": target}, device_id_type=MESH,
        )

    g_far, g_core, g_chip = g_copy(far, 1, core), g_copy(core, 0, core), g_copy(chip, 2, chip)
    g_far.start()
    v_chip.wait_recv()
    v_fwd = v_copy(chip, 2, core)
    v_fwd.start()
    g_core.start()
    g_far.wait_recv()
    for i in range(cells):
        igp[chip, i] = igp[chip, i] + rs[1, i]
    g_chip.start()

    v_core.wait_recv()
    for g in (col, chip, core):
        for i in range(cells):
            x2[g, i] = split(vx[g, i])
    v_fwd.wait_recv()
    for i in range(cells):
        x2[far, i] = split(vx[far, i])

    def block(z):
        return jnp.concatenate(
            [
                jnp.concatenate([x2[g, z * rows + x] for g in range(4)], axis=0)
                for x in range(rows)
            ],
            axis=1,
        )

    def weigh(z, total):
        return total + lax.dot_general(block(z), stack(z), nt, preferred_element_type=F32)

    total = lax.fori_loop(0, planes, weigh, jnp.zeros((64, 2 * taps8), F32))
    folded = jnp.concatenate(
        [total[g * 16 : g * 16 + 8] + total[g * 16 + 8 : g * 16 + 16] for g in range(4)], axis=0
    )
    wide = jnp.concatenate(
        [folded, jnp.zeros((32, 512 - 2 * taps8), F32)], axis=1
    )
    wide = jnp.concatenate([wide, jnp.zeros((96, 512), F32)], axis=0)
    for p in range(PIECES):
        if p % 2 == 0:
            turned = wide[:, (p // 2) * 128 : (p // 2 + 1) * 128].T
        tile = jnp.zeros((8, 128), F32)
        for q in range(4):
            at = (p % 2) * 64 + q * 16
            term = turned[at : at + 8] + turned[at + 8 : at + 16]
            tile = tile + (pltpu.roll(term, q * 32, 1) if q else term)
        gpack[p] = tile

    def s1_copy(i):
        return pltpu.make_async_remote_copy(
            src_ref=gpack.at[i], dst_ref=grecv.at[me], send_sem=s1_send.at[i],
            recv_sem=s1_recv.at[me], device_id={"gx": i // ny, "gy": i % ny}, device_id_type=MESH,
        )

    for i in range(PIECES):
        @pl.when(me != i)
        def _():
            s1_copy(i).start()

    acc[...] = jnp.zeros_like(acc)

    def forward(z, carry):
        cell = block(z)
        y = jnp.dot(w_fwd, jnp.concatenate([cell, cell], axis=0), preferred_element_type=F32)
        for a in range(3):
            for e in range(3):
                for x in range(rows + 2):
                    terms = [
                        y[
                            ((a * 3 + b) * 3 + e) * 8 : ((a * 3 + b) * 3 + e) * 8 + 8,
                            (x + b - 2) * 128 : (x + b - 1) * 128,
                        ]
                        for b in range(3)
                        if 0 <= x + b - 2 < rows
                    ]
                    acc[e, z + 2 - a, x] = functools.reduce(lambda s, t: s + t, terms, acc[e, z + 2 - a, x])
        return carry

    lax.fori_loop(0, planes, forward, 0)
    pack = jnp.zeros((8, 128), F32)
    for z in range(planes):
        for x in range(rows + 2):
            at = z * 8 + x
            up, down = acc[0, z + 1, x], acc[2, z + 1, x]
            pack = jnp.where(lane == at, pltpu.roll(up, at + 1, 1), pack)
            pack = jnp.where(lane == at + 64, pltpu.roll(down, at + 64, 1), pack)
            local[x, z] = (
                acc[1, z + 1, x]
                + jnp.where(lane == 0, 0.0, pltpu.roll(up, 1, 1))
                + jnp.where(lane == 127, 0.0, pltpu.roll(down, 127, 1))
            )
    rpack_out[...] = pack
    each(r_copy, "start", True)

    def s2_copy(i, j):
        return pltpu.make_async_remote_copy(
            src_ref=gfin.at[i], dst_ref=gfin.at[i], send_sem=s2_send.at[j],
            recv_sem=s2_recv.at[i], device_id={"gx": j // ny, "gy": j % ny}, device_id_type=MESH,
        )

    def s1_arrival(j):
        return pltpu.make_async_remote_copy(
            src_ref=gpack.at[0], dst_ref=grecv.at[j], send_sem=s1_send.at[0],
            recv_sem=s1_recv.at[j], device_id={"gx": j // ny, "gy": j % ny}, device_id_type=MESH,
        )

    @pl.when(me < PIECES)
    def _():
        grecv[me] = gpack[me]

        def collect(j, total):
            @pl.when(j != me)
            def _():
                s1_arrival(j).wait_recv()
            return total + grecv[j]

        gfin[me] = lax.fori_loop(0, group, collect, jnp.zeros((8, 128), F32)) * scale

        def hand_out(j, carry):
            @pl.when(j != me)
            def _():
                s2_copy(me, j).start()
            return carry

        lax.fori_loop(0, group, hand_out, 0)

    g_core.wait_recv()
    g_chip.wait_recv()
    for i in range(cells):
        grad_ref[pl.ds(i, 8, stride=cells), :] = igp[col, i] + rs[0, i] + rs[2, i]

    each(r_copy, "wait_recv", False)
    edge = jnp.zeros((8, 128), F32)
    for first, keep in ((3, lane < 64), (0, lane >= 64)):
        before, mid, after = rpack_in[first + 2], rpack_in[first + 1], rpack_in[first]
        total = mid + jnp.where(spot == 1, pltpu.roll(before, 128 - rows, 1), 0.0)
        total = total + jnp.where(spot == rows, pltpu.roll(after, rows, 1), 0.0)
        edge = jnp.where(keep, total, edge)
    for z in range(planes):
        for x in range(rows):
            at = z * 8 + x + 1
            tile = local[x + 1, z]
            if x == 0:
                tile = tile + row_in[1, z]
            if x == rows - 1:
                tile = tile + row_in[0, z]
            tile = tile + jnp.where(lane == 0, pltpu.roll(edge, 128 - at, 1), 0.0)
            tile = tile + jnp.where(lane == 127, pltpu.roll(edge, (127 - 64 - at) % 128, 1), 0.0)
            resp_ref[pl.ds(z * rows + x, 8, stride=cells), :] = tile

    for i in range(PIECES):
        @pl.when(me != i)
        def _():
            s2_copy(i, i).wait_recv()
        for q in range(4):
            if i * 4 + q < 27:
                tile = gfin[i]
                if q:
                    tile = pltpu.roll(tile, 128 - q * 32, 1)
                fg_ref[(i * 4 + q) * 8 : (i * 4 + q) * 8 + 8, :] = tile[:, :32]

    each(u_copy, "wait_send", True)
    each(r_copy, "wait_send", True)
    for copy in (v_chip, v_core, v_fwd, g_far, g_core, g_chip):
        copy.wait_send()
    for i in range(PIECES):
        @pl.when(me != i)
        def _():
            s1_copy(i).wait_send()

    @pl.when(me < PIECES)
    def _():
        def left(j, carry):
            @pl.when(j != me)
            def _():
                s2_copy(me, j).wait_send()
            return carry

        lax.fori_loop(0, group, left, 0)


def solution(mesh):
    nx, ny = mesh.shape["gx"], mesh.shape["gy"]

    def shards(volume, filters, upstream):
        own, planes, rows, width = volume.shape
        cells = planes * rows
        scale = (planes * rows * nx * width * ny) ** (-0.5)
        weights = filters.transpose(2, 3, 4, 0, 1).reshape(27 * own, 32)
        tile = (8, 128)
        resp, grad, fg = pl.pallas_call(
            functools.partial(kernel, nx, ny, planes, rows, scale),
            out_shape=(
                jax.ShapeDtypeStruct((own * cells, width), F32),
                jax.ShapeDtypeStruct((own * cells, width), F32),
                jax.ShapeDtypeStruct((27 * own, 32), F32),
            ),
            in_specs=[pl.BlockSpec(memory_space=pl.ANY)] * 3,
            out_specs=(pl.BlockSpec(memory_space=pltpu.VMEM),) * 3,
            scratch_shapes=[
                pltpu.VMEM((own * cells, width), F32),
                pltpu.VMEM((27 * own, 32), F32),
                pltpu.VMEM((own * cells, width), F32),
                pltpu.VMEM((4, cells) + tile, F32),
                pltpu.VMEM((4, cells, 16, 128), BF16),
                pltpu.VMEM((planes, rows) + tile, F32),
                pltpu.VMEM((2, planes) + tile, F32),
                pltpu.VMEM(tile, F32),
                pltpu.VMEM((6,) + tile, F32),
                pltpu.VMEM((3, planes + 2, rows + 2, 16, 128), BF16),
                pltpu.VMEM((4, cells) + tile, F32),
                pltpu.VMEM((3, cells) + tile, F32),
                pltpu.VMEM((3, planes + 2, rows + 2) + tile, F32),
                pltpu.VMEM((rows + 2, planes) + tile, F32),
                pltpu.VMEM((2, planes) + tile, F32),
                pltpu.VMEM(tile, F32),
                pltpu.VMEM((6,) + tile, F32),
                pltpu.VMEM((PIECES,) + tile, F32),
                pltpu.VMEM((nx * ny,) + tile, F32),
                pltpu.VMEM((PIECES,) + tile, F32),
                pltpu.SemaphoreType.DMA((3,)),
                pltpu.SemaphoreType.DMA((3,)),
                pltpu.SemaphoreType.DMA((3,)),
                pltpu.SemaphoreType.DMA((8,)),
                pltpu.SemaphoreType.DMA((8,)),
                pltpu.SemaphoreType.DMA((3,)),
                pltpu.SemaphoreType.DMA((3,)),
                pltpu.SemaphoreType.DMA((8,)),
                pltpu.SemaphoreType.DMA((8,)),
                pltpu.SemaphoreType.DMA((PIECES,)),
                pltpu.SemaphoreType.DMA((nx * ny,)),
                pltpu.SemaphoreType.DMA((nx * ny,)),
                pltpu.SemaphoreType.DMA((PIECES,)),
            ],
            compiler_params=pltpu.CompilerParams(
                collective_id=0, has_side_effects=True, vmem_limit_bytes=40 * 1024 * 1024
            ),
        )(
            volume.reshape(own * cells, width),
            weights,
            upstream.reshape(own * cells, width),
        )
        return (
            resp.reshape(volume.shape),
            grad.reshape(volume.shape),
            fg.reshape(3, 3, 3, own, 32).transpose(3, 4, 0, 1, 2),
        )

    return jax.shard_map(
        shards,
        mesh=mesh,
        in_specs=(
            P("col", None, "gx", "gy"),
            P("col", None, None, None, None),
            P("col", None, "gx", "gy"),
        ),
        out_specs=(
            P("col", None, "gx", "gy"),
            P("col", None, "gx", "gy"),
            P("col", None, None, None, None),
        ),
        check_vma=False,
    )
```

```python
import functools

import jax
import jax.numpy as jnp
from jax import lax
from jax.experimental import pallas as pl
from jax.experimental.pallas import tpu as pltpu
from jax.sharding import PartitionSpec as P

MESH = pl.DeviceIdType.MESH
F32 = jnp.float32
BF16 = jnp.bfloat16
DIRS = [(-1, 0), (1, 0), (-1, -1), (0, -1), (1, -1), (-1, 1), (0, 1), (1, 1)]
TAPS = [(a, b, e) for a in range(3) for b in range(3) for e in range(3)]
CHUNKS = 4
PIECES = 7


def split(value):
    high = value.astype(BF16).astype(F32)
    return jnp.concatenate([high, value - high], axis=0).astype(BF16)


def kernel(
    nx, ny, planes, rows, scale,
    v_hbm, w_hbm, u_hbm,
    resp_ref, grad_ref, fg_ref,
    v_in, w_in, u_in, vx, x2, u_own, u_row, pack_out, pack_in, u3, igp, rs,
    acc, local, row_in, rpack_out, rpack_in, gpack, grecv, gfin,
    in_sem, v_send, v_recv, u_send, u_recv, g_send, g_recv, r_send, r_recv,
    s1_send, s1_recv, s2_send, s2_recv,
):
    col, gx, gy = lax.axis_index("col"), lax.axis_index("gx"), lax.axis_index("gy")
    group = nx * ny
    me = gx * ny + gy
    cells = planes * rows
    span = cells // CHUNKS
    low, high = col % 2, col // 2
    core = high * 2 + (1 - low)
    chip = (1 - high) * 2 + low
    far = (1 - high) * 2 + (1 - low)

    def exists(dx, dy):
        ok = None
        for d, at, size in ((dx, gx, nx), (dy, gy, ny)):
            if d:
                term = (at + d >= 0) & (at + d < size)
                ok = term if ok is None else ok & term
        return ok

    loads = [
        pltpu.make_async_copy(s, d, in_sem.at[i])
        for i, (s, d) in enumerate(((v_hbm, v_in), (u_hbm, u_in), (w_hbm, w_in)))
    ]
    for load in loads:
        load.start()
    barrier = pltpu.get_barrier_semaphore()

    for other in (core, chip):
        pl.semaphore_signal(barrier, inc=1, device_id={"col": other}, device_id_type=MESH)

    def greet(j, carry):
        @pl.when(j != me)
        def _():
            pl.semaphore_signal(
                barrier, inc=1, device_id={"gx": j // ny, "gy": j % ny}, device_id_type=MESH
            )
        return carry

    lax.fori_loop(0, group, greet, 0)

    for d, (dx, dy) in enumerate(DIRS):
        @pl.when(jnp.logical_not(exists(-dx, -dy)))
        def _():
            for row, corner in ((u_row, pack_in), (row_in, rpack_in)):
                if dy == 0:
                    row[d] = jnp.zeros(row.shape[1:], F32)
                else:
                    corner[d - 2] = jnp.zeros((8, 128), F32)

    lane = lax.broadcasted_iota(jnp.int32, (8, 128), 1)
    loads[0].wait()
    for i in range(cells):
        vx[col, i] = v_in[pl.ds(i, 8, stride=cells), :]
    loads[1].wait()
    for i in range(cells):
        u_own[i // rows, i % rows] = u_in[pl.ds(i, 8, stride=cells), :]
    pack = jnp.zeros((8, 128), F32)
    for z in range(planes):
        for x in range(rows):
            at = z * 8 + x + 1
            tile = u_own[z, x]
            pack = jnp.where(lane == at, pltpu.roll(tile, at + 1, 1), pack)
            pack = jnp.where(lane == at + 64, pltpu.roll(tile, at + 64, 1), pack)
    pack_out[...] = pack

    pl.semaphore_wait(barrier, group + 1)

    def v_copy(slot, sem, target, k):
        part = vx.at[slot, pl.ds(k * span, span)]
        return pltpu.make_async_remote_copy(
            src_ref=part, dst_ref=part, send_sem=v_send.at[sem, k],
            recv_sem=v_recv.at[sem, k], device_id={"col": target}, device_id_type=MESH,
        )

    def u_copy(d):
        dx, dy = DIRS[d]
        if dy == 0:
            src = u_own.at[:, 0 if dx < 0 else rows - 1]
            dst = u_row.at[d]
        else:
            src, dst = pack_out, pack_in.at[d - 2]
        return pltpu.make_async_remote_copy(
            src_ref=src, dst_ref=dst, send_sem=u_send.at[d], recv_sem=u_recv.at[d],
            device_id={"gx": gx + dx, "gy": gy + dy}, device_id_type=MESH,
        )

    def r_copy(d):
        dx, dy = DIRS[d]
        if dy == 0:
            src, dst = local.at[0 if dx < 0 else rows + 1], row_in.at[d]
        else:
            src, dst = rpack_out, rpack_in.at[d - 2]
        return pltpu.make_async_remote_copy(
            src_ref=src, dst_ref=dst, send_sem=r_send.at[d], recv_sem=r_recv.at[d],
            device_id={"gx": gx + dx, "gy": gy + dy}, device_id_type=MESH,
        )

    def each(copies, what, sender):
        for d, (dx, dy) in enumerate(DIRS):
            @pl.when(exists(dx, dy) if sender else exists(-dx, -dy))
            def _():
                getattr(copies(d), what)()

    each(u_copy, "start", True)
    v_chip = [v_copy(col, 0, chip, k) for k in range(CHUNKS)]
    v_core = [v_copy(col, 1, core, k) for k in range(CHUNKS)]
    v_fwd = [v_copy(chip, 2, core, k) for k in range(CHUNKS)]
    for k in range(CHUNKS):
        v_chip[k].start()
        v_core[k].start()

    def hand_on(k):
        v_chip[k].wait_recv()
        v_fwd[k].start()

    loads[2].wait()
    w = w_in[...]
    taps8 = w.shape[0]
    w_hi = w.astype(BF16)
    w_lo = (w - w_hi.astype(F32)).astype(BF16)
    c_at = lax.broadcasted_iota(jnp.int32, (32, 128), 0)
    k_at = lax.broadcasted_iota(jnp.int32, (32, 128), 1)
    same = ((k_at % 64) // 16 == c_at // 8) & (k_at % 8 == c_at % 8)
    pick_hi = jnp.where(same & (k_at < 64), 1.0, 0.0).astype(BF16)
    pick_lo = jnp.where(same & (k_at >= 64), 1.0, 0.0).astype(BF16)
    w_fwd = (
        jnp.dot(w_hi, pick_hi, preferred_element_type=F32)
        + jnp.dot(w_lo, pick_lo, preferred_element_type=F32)
    ).astype(BF16)
    eye_r = lax.broadcasted_iota(jnp.int32, (32, 32), 0)
    eye_c = lax.broadcasted_iota(jnp.int32, (32, 32), 1)
    eye = jnp.where(eye_r == eye_c, 1.0, 0.0).astype(BF16)
    d_r = lax.broadcasted_iota(jnp.int32, (taps8, 2 * taps8), 0)
    d_c = lax.broadcasted_iota(jnp.int32, (taps8, 2 * taps8), 1)
    twice = jnp.where((d_r // 8 == d_c // 16) & (d_r % 8 == d_c % 8), 1.0, 0.0).astype(BF16)
    nt = (((1,), (1,)), ((), ()))
    w_back = []
    for part in (w_hi, w_lo):
        turned = lax.dot_general(eye, part, nt, preferred_element_type=F32).astype(BF16)
        w_back.append(jnp.dot(turned, twice, preferred_element_type=F32))
    w_back = jnp.concatenate(w_back, axis=0).astype(BF16)

    each(u_copy, "wait_recv", False)
    hand_on(0)
    spot = lane % 8
    edge = jnp.zeros((8, 128), F32)
    for first, keep in ((3, lane < 64), (0, lane >= 64)):
        before, mid, after = pack_in[first + 2], pack_in[first + 1], pack_in[first]
        total = jnp.where((spot >= 1) & (spot <= rows), mid, 0.0)
        total = jnp.where(spot == 0, pltpu.roll(before, 128 - rows, 1), total)
        total = jnp.where(spot == rows + 1, pltpu.roll(after, rows, 1), total)
        edge = jnp.where(keep, total, edge)
    zero16 = jnp.zeros((16, 128), BF16)
    for e in range(3):
        for x in range(rows + 2):
            u3[e, 0, x] = zero16
            u3[e, planes + 1, x] = zero16
    for z in range(planes):
        for x in range(rows + 2):
            at = z * 8 + x
            if x == 0:
                tile = u_row[1, z]
            elif x == rows + 1:
                tile = u_row[0, z]
            else:
                tile = u_own[z, x - 1]
            left = jnp.where(
                lane == 127, pltpu.roll(edge, (127 - 64 - at) % 128, 1), pltpu.roll(tile, 127, 1)
            )
            right = jnp.where(
                lane == 0, pltpu.roll(edge, (128 - at) % 128, 1), pltpu.roll(tile, 1, 1)
            )
            u3[0, z + 1, x] = split(left)
            u3[1, z + 1, x] = split(tile)
            u3[2, z + 1, x] = split(right)

    def stack(z):
        return jnp.concatenate(
            [
                jnp.concatenate([u3[e, z + 2 - a, x + 2 - b] for a, b, e in TAPS], axis=0)
                for x in range(rows)
            ],
            axis=1,
        )

    def back(z, carry):
        both = jnp.dot(w_back, stack(z), preferred_element_type=F32)
        for g in range(4):
            for x in range(rows):
                lanes = slice(x * 128, (x + 1) * 128)
                igp[g, z * rows + x] = (
                    both[g * 8 : g * 8 + 8, lanes] + both[32 + g * 8 : 40 + g * 8, lanes]
                )
        return carry

    hand_on(1)
    lax.fori_loop(0, planes // 2, back, 0)
    hand_on(2)
    lax.fori_loop(planes // 2, planes, back, 0)

    def g_copy(slot, to, target):
        return pltpu.make_async_remote_copy(
            src_ref=igp.at[slot], dst_ref=rs.at[to], send_sem=g_send.at[to],
            recv_sem=g_recv.at[to], device_id={"col": target}, device_id_type=MESH,
        )

    g_far, g_core, g_chip = g_copy(far, 1, core), g_copy(core, 0, core), g_copy(chip, 2, chip)
    g_far.start()
    hand_on(3)
    g_core.start()
    g_far.wait_recv()
    for i in range(cells):
        igp[chip, i] = igp[chip, i] + rs[1, i]
    g_chip.start()

    def block(z):
        return jnp.concatenate(
            [
                jnp.concatenate([x2[g, z * rows + x] for g in range(4)], axis=0)
                for x in range(rows)
            ],
            axis=1,
        )

    def weigh(z, total):
        return total + lax.dot_general(block(z), stack(z), nt, preferred_element_type=F32)

    total = jnp.zeros((64, 2 * taps8), F32)
    for k in range(CHUNKS):
        v_core[k].wait_recv()
        for g in (col, chip, core):
            for i in range(k * span, (k + 1) * span):
                x2[g, i] = split(vx[g, i])
        v_fwd[k].wait_recv()
        for i in range(k * span, (k + 1) * span):
            x2[far, i] = split(vx[far, i])
        total = lax.fori_loop(k * planes // CHUNKS, (k + 1) * planes // CHUNKS, weigh, total)
    folded = jnp.concatenate(
        [total[g * 16 : g * 16 + 8] + total[g * 16 + 8 : g * 16 + 16] for g in range(4)], axis=0
    )
    wide = jnp.concatenate(
        [folded, jnp.zeros((32, 512 - 2 * taps8), F32)], axis=1
    )
    wide = jnp.concatenate([wide, jnp.zeros((96, 512), F32)], axis=0)
    for p in range(PIECES):
        if p % 2 == 0:
            turned = wide[:, (p // 2) * 128 : (p // 2 + 1) * 128].T
        tile = jnp.zeros((8, 128), F32)
        for q in range(4):
            at = (p % 2) * 64 + q * 16
            term = turned[at : at + 8] + turned[at + 8 : at + 16]
            tile = tile + (pltpu.roll(term, q * 32, 1) if q else term)
        gpack[p] = tile

    def s1_copy(i):
        return pltpu.make_async_remote_copy(
            src_ref=gpack.at[i], dst_ref=grecv.at[me], send_sem=s1_send.at[i],
            recv_sem=s1_recv.at[me], device_id={"gx": i // ny, "gy": i % ny}, device_id_type=MESH,
        )

    for i in range(PIECES):
        @pl.when(me != i)
        def _():
            s1_copy(i).start()

    acc[...] = jnp.zeros_like(acc)

    def forward(z, carry):
        cell = block(z)
        y = jnp.dot(w_fwd, jnp.concatenate([cell, cell], axis=0), preferred_element_type=F32)
        for a in range(3):
            for e in range(3):
                for x in range(rows + 2):
                    terms = [
                        y[
                            ((a * 3 + b) * 3 + e) * 8 : ((a * 3 + b) * 3 + e) * 8 + 8,
                            (x + b - 2) * 128 : (x + b - 1) * 128,
                        ]
                        for b in range(3)
                        if 0 <= x + b - 2 < rows
                    ]
                    acc[e, z + 2 - a, x] = functools.reduce(lambda s, t: s + t, terms, acc[e, z + 2 - a, x])
        return carry

    lax.fori_loop(0, planes, forward, 0)
    pack = jnp.zeros((8, 128), F32)
    for z in range(planes):
        for x in range(rows + 2):
            at = z * 8 + x
            up, down = acc[0, z + 1, x], acc[2, z + 1, x]
            pack = jnp.where(lane == at, pltpu.roll(up, at + 1, 1), pack)
            pack = jnp.where(lane == at + 64, pltpu.roll(down, at + 64, 1), pack)
            local[x, z] = (
                acc[1, z + 1, x]
                + jnp.where(lane == 0, 0.0, pltpu.roll(up, 1, 1))
                + jnp.where(lane == 127, 0.0, pltpu.roll(down, 127, 1))
            )
    rpack_out[...] = pack
    each(r_copy, "start", True)

    def s2_copy(i, j):
        return pltpu.make_async_remote_copy(
            src_ref=gfin.at[i], dst_ref=gfin.at[i], send_sem=s2_send.at[j],
            recv_sem=s2_recv.at[i], device_id={"gx": j // ny, "gy": j % ny}, device_id_type=MESH,
        )

    def s1_arrival(j):
        return pltpu.make_async_remote_copy(
            src_ref=gpack.at[0], dst_ref=grecv.at[j], send_sem=s1_send.at[0],
            recv_sem=s1_recv.at[j], device_id={"gx": j // ny, "gy": j % ny}, device_id_type=MESH,
        )

    @pl.when(me < PIECES)
    def _():
        grecv[me] = gpack[me]

        def collect(j, total):
            @pl.when(j != me)
            def _():
                s1_arrival(j).wait_recv()
            return total + grecv[j]

        gfin[me] = lax.fori_loop(0, group, collect, jnp.zeros((8, 128), F32)) * scale

        def hand_out(j, carry):
            @pl.when(j != me)
            def _():
                s2_copy(me, j).start()
            return carry

        lax.fori_loop(0, group, hand_out, 0)

    g_core.wait_recv()
    g_chip.wait_recv()
    for i in range(cells):
        grad_ref[pl.ds(i, 8, stride=cells), :] = igp[col, i] + rs[0, i] + rs[2, i]

    each(r_copy, "wait_recv", False)
    edge = jnp.zeros((8, 128), F32)
    for first, keep in ((3, lane < 64), (0, lane >= 64)):
        before, mid, after = rpack_in[first + 2], rpack_in[first + 1], rpack_in[first]
        total = mid + jnp.where(spot == 1, pltpu.roll(before, 128 - rows, 1), 0.0)
        total = total + jnp.where(spot == rows, pltpu.roll(after, rows, 1), 0.0)
        edge = jnp.where(keep, total, edge)
    for z in range(planes):
        for x in range(rows):
            at = z * 8 + x + 1
            tile = local[x + 1, z]
            if x == 0:
                tile = tile + row_in[1, z]
            if x == rows - 1:
                tile = tile + row_in[0, z]
            tile = tile + jnp.where(lane == 0, pltpu.roll(edge, 128 - at, 1), 0.0)
            tile = tile + jnp.where(lane == 127, pltpu.roll(edge, (127 - 64 - at) % 128, 1), 0.0)
            resp_ref[pl.ds(z * rows + x, 8, stride=cells), :] = tile

    for i in range(PIECES):
        @pl.when(me != i)
        def _():
            s2_copy(i, i).wait_recv()
        for q in range(4):
            if i * 4 + q < 27:
                tile = gfin[i]
                if q:
                    tile = pltpu.roll(tile, 128 - q * 32, 1)
                fg_ref[(i * 4 + q) * 8 : (i * 4 + q) * 8 + 8, :] = tile[:, :32]

    each(u_copy, "wait_send", True)
    each(r_copy, "wait_send", True)
    for copy in (*v_chip, *v_core, *v_fwd, g_far, g_core, g_chip):
        copy.wait_send()
    for i in range(PIECES):
        @pl.when(me != i)
        def _():
            s1_copy(i).wait_send()

    @pl.when(me < PIECES)
    def _():
        def left(j, carry):
            @pl.when(j != me)
            def _():
                s2_copy(me, j).wait_send()
            return carry

        lax.fori_loop(0, group, left, 0)


def solution(mesh):
    nx, ny = mesh.shape["gx"], mesh.shape["gy"]

    def shards(volume, filters, upstream):
        own, planes, rows, width = volume.shape
        cells = planes * rows
        scale = (planes * rows * nx * width * ny) ** (-0.5)
        weights = filters.transpose(2, 3, 4, 0, 1).reshape(27 * own, 32)
        tile = (8, 128)
        resp, grad, fg = pl.pallas_call(
            functools.partial(kernel, nx, ny, planes, rows, scale),
            out_shape=(
                jax.ShapeDtypeStruct((own * cells, width), F32),
                jax.ShapeDtypeStruct((own * cells, width), F32),
                jax.ShapeDtypeStruct((27 * own, 32), F32),
            ),
            in_specs=[pl.BlockSpec(memory_space=pl.ANY)] * 3,
            out_specs=(pl.BlockSpec(memory_space=pltpu.VMEM),) * 3,
            scratch_shapes=[
                pltpu.VMEM((own * cells, width), F32),
                pltpu.VMEM((27 * own, 32), F32),
                pltpu.VMEM((own * cells, width), F32),
                pltpu.VMEM((4, cells) + tile, F32),
                pltpu.VMEM((4, cells, 16, 128), BF16),
                pltpu.VMEM((planes, rows) + tile, F32),
                pltpu.VMEM((2, planes) + tile, F32),
                pltpu.VMEM(tile, F32),
                pltpu.VMEM((6,) + tile, F32),
                pltpu.VMEM((3, planes + 2, rows + 2, 16, 128), BF16),
                pltpu.VMEM((4, cells) + tile, F32),
                pltpu.VMEM((3, cells) + tile, F32),
                pltpu.VMEM((3, planes + 2, rows + 2) + tile, F32),
                pltpu.VMEM((rows + 2, planes) + tile, F32),
                pltpu.VMEM((2, planes) + tile, F32),
                pltpu.VMEM(tile, F32),
                pltpu.VMEM((6,) + tile, F32),
                pltpu.VMEM((PIECES,) + tile, F32),
                pltpu.VMEM((nx * ny,) + tile, F32),
                pltpu.VMEM((PIECES,) + tile, F32),
                pltpu.SemaphoreType.DMA((3,)),
                pltpu.SemaphoreType.DMA((3, CHUNKS)),
                pltpu.SemaphoreType.DMA((3, CHUNKS)),
                pltpu.SemaphoreType.DMA((8,)),
                pltpu.SemaphoreType.DMA((8,)),
                pltpu.SemaphoreType.DMA((3,)),
                pltpu.SemaphoreType.DMA((3,)),
                pltpu.SemaphoreType.DMA((8,)),
                pltpu.SemaphoreType.DMA((8,)),
                pltpu.SemaphoreType.DMA((PIECES,)),
                pltpu.SemaphoreType.DMA((nx * ny,)),
                pltpu.SemaphoreType.DMA((nx * ny,)),
                pltpu.SemaphoreType.DMA((PIECES,)),
            ],
            compiler_params=pltpu.CompilerParams(
                collective_id=0, has_side_effects=True, vmem_limit_bytes=63 * 1024 * 1024
            ),
        )(
            volume.reshape(own * cells, width),
            weights,
            upstream.reshape(own * cells, width),
        )
        return (
            resp.reshape(volume.shape),
            grad.reshape(volume.shape),
            fg.reshape(3, 3, 3, own, 32).transpose(3, 4, 0, 1, 2),
        )

    return jax.shard_map(
        shards,
        mesh=mesh,
        in_specs=(
            P("col", None, "gx", "gy"),
            P("col", None, None, None, None),
            P("col", None, "gx", "gy"),
        ),
        out_specs=(
            P("col", None, "gx", "gy"),
            P("col", None, "gx", "gy"),
            P("col", None, None, None, None),
        ),
        check_vma=False,
    )
```

```python
import functools

import jax
import jax.numpy as jnp
from jax import lax
from jax.experimental import pallas as pl
from jax.experimental.pallas import tpu as pltpu
from jax.sharding import PartitionSpec as P

MESH = pl.DeviceIdType.MESH
F32 = jnp.float32
BF16 = jnp.bfloat16
DIRS = [(-1, 0), (1, 0), (-1, -1), (0, -1), (1, -1), (-1, 1), (0, 1), (1, 1)]
TAPS = [(a, b, e) for a in range(3) for b in range(3) for e in range(3)]
CHUNKS = 4
PIECES = 8


def split(value):
    high = value.astype(BF16).astype(F32)
    return jnp.concatenate([high, value - high], axis=0).astype(BF16)


def kernel(
    nx, ny, planes, rows, scale,
    v_hbm, w_hbm, u_hbm,
    resp_ref, grad_ref, fg_ref,
    v_in, w_in, u_in, vx, x2, u_own, u_row, pack_out, pack_in, u3, igp, rs,
    acc, local, row_in, rpack_out, rpack_in, gpack, ybuf, zbuf, gfin,
    in_sem, v_send, v_recv, u_send, u_recv, g_send, g_recv, r_send, r_recv,
    y1_send, y1_recv, z_send, z_recv, y2_send, y2_recv,
):
    col, gx, gy = lax.axis_index("col"), lax.axis_index("gx"), lax.axis_index("gy")
    group = nx * ny
    me = gx * ny + gy
    cells = planes * rows
    span = cells // CHUNKS
    low, high = col % 2, col // 2
    core = high * 2 + (1 - low)
    chip = (1 - high) * 2 + low
    far = (1 - high) * 2 + (1 - low)

    def exists(dx, dy):
        ok = None
        for d, at, size in ((dx, gx, nx), (dy, gy, ny)):
            if d:
                term = (at + d >= 0) & (at + d < size)
                ok = term if ok is None else ok & term
        return ok

    loads = [
        pltpu.make_async_copy(s, d, in_sem.at[i])
        for i, (s, d) in enumerate(((v_hbm, v_in), (u_hbm, u_in), (w_hbm, w_in)))
    ]
    for load in loads:
        load.start()
    barrier = pltpu.get_barrier_semaphore()

    for other in (core, chip):
        pl.semaphore_signal(barrier, inc=1, device_id={"col": other}, device_id_type=MESH)

    def greet(j, carry):
        @pl.when(j != me)
        def _():
            pl.semaphore_signal(
                barrier, inc=1, device_id={"gx": j // ny, "gy": j % ny}, device_id_type=MESH
            )
        return carry

    lax.fori_loop(0, group, greet, 0)

    for d, (dx, dy) in enumerate(DIRS):
        @pl.when(jnp.logical_not(exists(-dx, -dy)))
        def _():
            for row, corner in ((u_row, pack_in), (row_in, rpack_in)):
                if dy == 0:
                    row[d] = jnp.zeros(row.shape[1:], F32)
                else:
                    corner[d - 2] = jnp.zeros((8, 128), F32)

    lane = lax.broadcasted_iota(jnp.int32, (8, 128), 1)
    loads[0].wait()
    for i in range(cells):
        vx[col, i] = v_in[pl.ds(i, 8, stride=cells), :]
    loads[1].wait()
    for i in range(cells):
        u_own[i // rows, i % rows] = u_in[pl.ds(i, 8, stride=cells), :]
    pack = jnp.zeros((8, 128), F32)
    for z in range(planes):
        for x in range(rows):
            at = z * 8 + x + 1
            tile = u_own[z, x]
            pack = jnp.where(lane == at, pltpu.roll(tile, at + 1, 1), pack)
            pack = jnp.where(lane == at + 64, pltpu.roll(tile, at + 64, 1), pack)
    pack_out[...] = pack

    pl.semaphore_wait(barrier, group + 1)

    def v_copy(slot, sem, target, k):
        part = vx.at[slot, pl.ds(k * span, span)]
        return pltpu.make_async_remote_copy(
            src_ref=part, dst_ref=part, send_sem=v_send.at[sem, k],
            recv_sem=v_recv.at[sem, k], device_id={"col": target}, device_id_type=MESH,
        )

    def u_copy(d):
        dx, dy = DIRS[d]
        if dy == 0:
            src = u_own.at[:, 0 if dx < 0 else rows - 1]
            dst = u_row.at[d]
        else:
            src, dst = pack_out, pack_in.at[d - 2]
        return pltpu.make_async_remote_copy(
            src_ref=src, dst_ref=dst, send_sem=u_send.at[d], recv_sem=u_recv.at[d],
            device_id={"gx": gx + dx, "gy": gy + dy}, device_id_type=MESH,
        )

    def r_copy(d):
        dx, dy = DIRS[d]
        if dy == 0:
            src, dst = local.at[0 if dx < 0 else rows + 1], row_in.at[d]
        else:
            src, dst = rpack_out, rpack_in.at[d - 2]
        return pltpu.make_async_remote_copy(
            src_ref=src, dst_ref=dst, send_sem=r_send.at[d], recv_sem=r_recv.at[d],
            device_id={"gx": gx + dx, "gy": gy + dy}, device_id_type=MESH,
        )

    def each(copies, what, sender):
        for d, (dx, dy) in enumerate(DIRS):
            @pl.when(exists(dx, dy) if sender else exists(-dx, -dy))
            def _():
                getattr(copies(d), what)()

    each(u_copy, "start", True)
    v_chip = [v_copy(col, 0, chip, k) for k in range(CHUNKS)]
    v_core = [v_copy(col, 1, core, k) for k in range(CHUNKS)]
    v_fwd = [v_copy(chip, 2, core, k) for k in range(CHUNKS)]
    for k in range(CHUNKS):
        v_chip[k].start()
        v_core[k].start()

    def hand_on(k):
        v_chip[k].wait_recv()
        v_fwd[k].start()

    loads[2].wait()
    w = w_in[...]
    taps8 = w.shape[0]
    w_hi = w.astype(BF16)
    w_lo = (w - w_hi.astype(F32)).astype(BF16)
    c_at = lax.broadcasted_iota(jnp.int32, (32, 128), 0)
    k_at = lax.broadcasted_iota(jnp.int32, (32, 128), 1)
    same = k_at % 32 == c_at
    pick_hi = jnp.where(same & (k_at < 64), 1.0, 0.0).astype(BF16)
    pick_lo = jnp.where(same & (k_at >= 64), 1.0, 0.0).astype(BF16)
    w_fwd = (
        jnp.dot(w_hi, pick_hi, preferred_element_type=F32)
        + jnp.dot(w_lo, pick_lo, preferred_element_type=F32)
    ).astype(BF16)
    eye_r = lax.broadcasted_iota(jnp.int32, (32, 32), 0)
    eye_c = lax.broadcasted_iota(jnp.int32, (32, 32), 1)
    eye = jnp.where(eye_r == eye_c, 1.0, 0.0).astype(BF16)
    d_r = lax.broadcasted_iota(jnp.int32, (taps8, 2 * taps8), 0)
    d_c = lax.broadcasted_iota(jnp.int32, (taps8, 2 * taps8), 1)
    twice = jnp.where((d_r // 8 == d_c // 16) & (d_r % 8 == d_c % 8), 1.0, 0.0).astype(BF16)
    nt = (((1,), (1,)), ((), ()))
    w_back = []
    for part in (w_hi, w_lo):
        turned = lax.dot_general(eye, part, nt, preferred_element_type=F32).astype(BF16)
        w_back.append(jnp.dot(turned, twice, preferred_element_type=F32))
    w_back = jnp.concatenate(w_back, axis=0).astype(BF16)

    each(u_copy, "wait_recv", False)
    hand_on(0)
    spot = lane % 8
    edge = jnp.zeros((8, 128), F32)
    for first, keep in ((3, lane < 64), (0, lane >= 64)):
        before, mid, after = pack_in[first + 2], pack_in[first + 1], pack_in[first]
        total = jnp.where((spot >= 1) & (spot <= rows), mid, 0.0)
        total = jnp.where(spot == 0, pltpu.roll(before, 128 - rows, 1), total)
        total = jnp.where(spot == rows + 1, pltpu.roll(after, rows, 1), total)
        edge = jnp.where(keep, total, edge)
    zero16 = jnp.zeros((16, 128), BF16)
    for e in range(3):
        for x in range(rows + 2):
            u3[e, 0, x] = zero16
            u3[e, planes + 1, x] = zero16
    for z in range(planes):
        for x in range(rows + 2):
            at = z * 8 + x
            if x == 0:
                tile = u_row[1, z]
            elif x == rows + 1:
                tile = u_row[0, z]
            else:
                tile = u_own[z, x - 1]
            left = jnp.where(
                lane == 127, pltpu.roll(edge, (127 - 64 - at) % 128, 1), pltpu.roll(tile, 127, 1)
            )
            right = jnp.where(
                lane == 0, pltpu.roll(edge, (128 - at) % 128, 1), pltpu.roll(tile, 1, 1)
            )
            u3[0, z + 1, x] = split(left)
            u3[1, z + 1, x] = split(tile)
            u3[2, z + 1, x] = split(right)

    def stack(z):
        return jnp.concatenate(
            [
                jnp.concatenate([u3[e, z + 2 - a, x + 2 - b] for a, b, e in TAPS], axis=0)
                for x in range(rows)
            ],
            axis=1,
        )

    def back(z, carry):
        both = jnp.dot(w_back, stack(z), preferred_element_type=F32)
        for g in range(4):
            for x in range(rows):
                lanes = slice(x * 128, (x + 1) * 128)
                igp[g, z * rows + x] = (
                    both[g * 8 : g * 8 + 8, lanes] + both[32 + g * 8 : 40 + g * 8, lanes]
                )
        return carry

    hand_on(1)
    lax.fori_loop(0, planes // 2, back, 0)
    hand_on(2)
    lax.fori_loop(planes // 2, planes, back, 0)

    def g_copy(slot, to, target):
        return pltpu.make_async_remote_copy(
            src_ref=igp.at[slot], dst_ref=rs.at[to], send_sem=g_send.at[to],
            recv_sem=g_recv.at[to], device_id={"col": target}, device_id_type=MESH,
        )

    g_far, g_core, g_chip = g_copy(far, 1, core), g_copy(core, 0, core), g_copy(chip, 2, chip)
    g_far.start()
    hand_on(3)
    g_core.start()
    g_far.wait_recv()
    for i in range(cells):
        igp[chip, i] = igp[chip, i] + rs[1, i]
    g_chip.start()

    def settle(q, i):
        tile = jnp.concatenate([vx[2 * q, i], vx[2 * q + 1, i]], axis=0)
        rounded = tile.astype(BF16)
        x2[0, q, i] = rounded
        x2[1, q, i] = (tile - rounded.astype(F32)).astype(BF16)

    def block(z):
        return jnp.concatenate(
            [
                jnp.concatenate(
                    [x2[h, q, z * rows + x] for h in range(2) for q in range(2)], axis=0
                )
                for x in range(rows)
            ],
            axis=1,
        )

    total = jnp.zeros((2 * taps8, 64), F32)
    for k in range(CHUNKS):
        v_core[k].wait_recv()
        for i in range(k * span, (k + 1) * span):
            settle(high, i)
        v_fwd[k].wait_recv()
        for i in range(k * span, (k + 1) * span):
            settle(1 - high, i)
        part = range(k * planes // CHUNKS, (k + 1) * planes // CHUNKS)
        total = total + lax.dot_general(
            jnp.concatenate([stack(z) for z in part], axis=1),
            jnp.concatenate([block(z) for z in part], axis=1),
            nt,
            preferred_element_type=F32,
        )
    for p in range(PIECES):
        tile = jnp.zeros((8, 128), F32)
        for q in range(4):
            t = p * 4 + q
            if t < 27:
                term = total[t * 16 : t * 16 + 8] + total[t * 16 + 8 : t * 16 + 16]
                term = jnp.concatenate([term, jnp.zeros((8, 64), F32)], axis=1)
                term = jnp.where(lane < 32, term + pltpu.roll(term, 96, 1), 0.0)
                tile = tile + (pltpu.roll(term, q * 32, 1) if q else term)
        gpack[p] = tile

    per = PIECES // ny

    def y1_copy(j):
        return pltpu.make_async_remote_copy(
            src_ref=gpack.at[pl.ds(j * per, per)], dst_ref=ybuf.at[gy], send_sem=y1_send.at[j],
            recv_sem=y1_recv.at[gy], device_id={"gy": j}, device_id_type=MESH,
        )

    def y1_arrival(j):
        return pltpu.make_async_remote_copy(
            src_ref=gpack.at[pl.ds(j * per, per)], dst_ref=ybuf.at[j], send_sem=y1_send.at[j],
            recv_sem=y1_recv.at[j], device_id={"gy": j}, device_id_type=MESH,
        )

    def z_copy(i):
        return pltpu.make_async_remote_copy(
            src_ref=zbuf.at[gx], dst_ref=zbuf.at[gx], send_sem=z_send.at[i],
            recv_sem=z_recv.at[gx], device_id={"gx": i}, device_id_type=MESH,
        )

    def z_arrival(i):
        return pltpu.make_async_remote_copy(
            src_ref=zbuf.at[i], dst_ref=zbuf.at[i], send_sem=z_send.at[i],
            recv_sem=z_recv.at[i], device_id={"gx": i}, device_id_type=MESH,
        )

    def y2_copy(j, part):
        place = gfin.at[pl.ds(part * per, per)]
        return pltpu.make_async_remote_copy(
            src_ref=place, dst_ref=place, send_sem=y2_send.at[j],
            recv_sem=y2_recv.at[part], device_id={"gy": j}, device_id_type=MESH,
        )

    def others(size, own, what):
        for j in range(size):
            @pl.when(own != j)
            def _():
                what(j)

    others(ny, gy, lambda j: y1_copy(j).start())
    ybuf[gy] = gpack[pl.ds(gy * per, per)]

    acc[...] = jnp.zeros_like(acc)

    def forward(z, carry):
        cell = block(z)
        y = jnp.dot(w_fwd, jnp.concatenate([cell, cell], axis=0), preferred_element_type=F32)
        for a in range(3):
            for e in range(3):
                for x in range(rows + 2):
                    terms = [
                        y[
                            ((a * 3 + b) * 3 + e) * 8 : ((a * 3 + b) * 3 + e) * 8 + 8,
                            (x + b - 2) * 128 : (x + b - 1) * 128,
                        ]
                        for b in range(3)
                        if 0 <= x + b - 2 < rows
                    ]
                    acc[e, z + 2 - a, x] = functools.reduce(lambda s, t: s + t, terms, acc[e, z + 2 - a, x])
        return carry

    def sum_y():
        others(ny, gy, lambda j: y1_arrival(j).wait_recv())
        zbuf[gx] = functools.reduce(lambda p, q: p + q, [ybuf[j] for j in range(ny)])
        others(nx, gx, lambda i: z_copy(i).start())

    lax.fori_loop(0, planes // 2, forward, 0)
    sum_y()
    lax.fori_loop(planes // 2, planes, forward, 0)
    pack = jnp.zeros((8, 128), F32)
    for z in range(planes):
        for x in range(rows + 2):
            at = z * 8 + x
            up, down = acc[0, z + 1, x], acc[2, z + 1, x]
            pack = jnp.where(lane == at, pltpu.roll(up, at + 1, 1), pack)
            pack = jnp.where(lane == at + 64, pltpu.roll(down, at + 64, 1), pack)
            local[x, z] = (
                acc[1, z + 1, x]
                + jnp.where(lane == 0, 0.0, pltpu.roll(up, 1, 1))
                + jnp.where(lane == 127, 0.0, pltpu.roll(down, 127, 1))
            )
    rpack_out[...] = pack
    each(r_copy, "start", True)

    others(nx, gx, lambda i: z_arrival(i).wait_recv())
    gfin[pl.ds(gy * per, per)] = (
        functools.reduce(lambda p, q: p + q, [zbuf[i] for i in range(nx)]) * scale
    )
    others(ny, gy, lambda j: y2_copy(j, gy).start())

    g_core.wait_recv()
    g_chip.wait_recv()
    for i in range(cells):
        grad_ref[pl.ds(i, 8, stride=cells), :] = igp[col, i] + rs[0, i] + rs[2, i]

    each(r_copy, "wait_recv", False)
    edge = jnp.zeros((8, 128), F32)
    for first, keep in ((3, lane < 64), (0, lane >= 64)):
        before, mid, after = rpack_in[first + 2], rpack_in[first + 1], rpack_in[first]
        total = mid + jnp.where(spot == 1, pltpu.roll(before, 128 - rows, 1), 0.0)
        total = total + jnp.where(spot == rows, pltpu.roll(after, rows, 1), 0.0)
        edge = jnp.where(keep, total, edge)
    for z in range(planes):
        for x in range(rows):
            at = z * 8 + x + 1
            tile = local[x + 1, z]
            if x == 0:
                tile = tile + row_in[1, z]
            if x == rows - 1:
                tile = tile + row_in[0, z]
            tile = tile + jnp.where(lane == 0, pltpu.roll(edge, 128 - at, 1), 0.0)
            tile = tile + jnp.where(lane == 127, pltpu.roll(edge, (127 - 64 - at) % 128, 1), 0.0)
            resp_ref[pl.ds(z * rows + x, 8, stride=cells), :] = tile

    others(ny, gy, lambda j: y2_copy(j, j).wait_recv())
    for i in range(PIECES):
        for q in range(4):
            if i * 4 + q < 27:
                tile = gfin[i]
                if q:
                    tile = pltpu.roll(tile, 128 - q * 32, 1)
                fg_ref[(i * 4 + q) * 8 : (i * 4 + q) * 8 + 8, :] = tile[:, :32]

    each(u_copy, "wait_send", True)
    each(r_copy, "wait_send", True)
    for copy in (*v_chip, *v_core, *v_fwd, g_far, g_core, g_chip):
        copy.wait_send()
    others(ny, gy, lambda j: y1_copy(j).wait_send())
    others(nx, gx, lambda i: z_copy(i).wait_send())
    others(ny, gy, lambda j: y2_copy(j, gy).wait_send())


def solution(mesh):
    nx, ny = mesh.shape["gx"], mesh.shape["gy"]

    def shards(volume, filters, upstream):
        own, planes, rows, width = volume.shape
        cells = planes * rows
        scale = (planes * rows * nx * width * ny) ** (-0.5)
        weights = filters.transpose(2, 3, 4, 0, 1).reshape(27 * own, 32)
        tile = (8, 128)
        resp, grad, fg = pl.pallas_call(
            functools.partial(kernel, nx, ny, planes, rows, scale),
            out_shape=(
                jax.ShapeDtypeStruct((own * cells, width), F32),
                jax.ShapeDtypeStruct((own * cells, width), F32),
                jax.ShapeDtypeStruct((27 * own, 32), F32),
            ),
            in_specs=[pl.BlockSpec(memory_space=pl.ANY)] * 3,
            out_specs=(pl.BlockSpec(memory_space=pltpu.VMEM),) * 3,
            scratch_shapes=[
                pltpu.VMEM((own * cells, width), F32),
                pltpu.VMEM((27 * own, 32), F32),
                pltpu.VMEM((own * cells, width), F32),
                pltpu.VMEM((4, cells) + tile, F32),
                pltpu.VMEM((2, 2, cells, 16, 128), BF16),
                pltpu.VMEM((planes, rows) + tile, F32),
                pltpu.VMEM((2, planes) + tile, F32),
                pltpu.VMEM(tile, F32),
                pltpu.VMEM((6,) + tile, F32),
                pltpu.VMEM((3, planes + 2, rows + 2, 16, 128), BF16),
                pltpu.VMEM((4, cells) + tile, F32),
                pltpu.VMEM((3, cells) + tile, F32),
                pltpu.VMEM((3, planes + 2, rows + 2) + tile, F32),
                pltpu.VMEM((rows + 2, planes) + tile, F32),
                pltpu.VMEM((2, planes) + tile, F32),
                pltpu.VMEM(tile, F32),
                pltpu.VMEM((6,) + tile, F32),
                pltpu.VMEM((PIECES,) + tile, F32),
                pltpu.VMEM((ny, PIECES // ny) + tile, F32),
                pltpu.VMEM((nx, PIECES // ny) + tile, F32),
                pltpu.VMEM((PIECES,) + tile, F32),
                pltpu.SemaphoreType.DMA((3,)),
                pltpu.SemaphoreType.DMA((3, CHUNKS)),
                pltpu.SemaphoreType.DMA((3, CHUNKS)),
                pltpu.SemaphoreType.DMA((8,)),
                pltpu.SemaphoreType.DMA((8,)),
                pltpu.SemaphoreType.DMA((3,)),
                pltpu.SemaphoreType.DMA((3,)),
                pltpu.SemaphoreType.DMA((8,)),
                pltpu.SemaphoreType.DMA((8,)),
                pltpu.SemaphoreType.DMA((ny,)),
                pltpu.SemaphoreType.DMA((ny,)),
                pltpu.SemaphoreType.DMA((nx,)),
                pltpu.SemaphoreType.DMA((nx,)),
                pltpu.SemaphoreType.DMA((ny,)),
                pltpu.SemaphoreType.DMA((ny,)),
            ],
            compiler_params=pltpu.CompilerParams(
                collective_id=0, has_side_effects=True, vmem_limit_bytes=63 * 1024 * 1024
            ),
        )(
            volume.reshape(own * cells, width),
            weights,
            upstream.reshape(own * cells, width),
        )
        return (
            resp.reshape(volume.shape),
            grad.reshape(volume.shape),
            fg.reshape(3, 3, 3, own, 32).transpose(3, 4, 0, 1, 2),
        )

    return jax.shard_map(
        shards,
        mesh=mesh,
        in_specs=(
            P("col", None, "gx", "gy"),
            P("col", None, None, None, None),
            P("col", None, "gx", "gy"),
        ),
        out_specs=(
            P("col", None, "gx", "gy"),
            P("col", None, "gx", "gy"),
            P("col", None, None, None, None),
        ),
        check_vma=False,
    )
```

```python
import functools

import jax
import jax.numpy as jnp
from jax import lax
from jax.experimental import pallas as pl
from jax.experimental.pallas import tpu as pltpu
from jax.sharding import PartitionSpec as P

MESH = pl.DeviceIdType.MESH
F32 = jnp.float32
BF16 = jnp.bfloat16
DIRS = [(-1, 0), (1, 0), (-1, -1), (0, -1), (1, -1), (-1, 1), (0, 1), (1, 1)]
TAPS = [(a, b, e) for a in range(3) for b in range(3) for e in range(3)]
CHUNKS = 4
PIECES = 7


def split(value):
    high = value.astype(BF16).astype(F32)
    return jnp.concatenate([high, value - high], axis=0).astype(BF16)


def kernel(
    nx, ny, planes, rows, scale,
    v_hbm, w_hbm, u_hbm,
    resp_ref, grad_ref, fg_ref,
    v_in, w_in, u_in, vx, x2, u_own, u_row, pack_out, pack_in, u3, igp, rs,
    acc, local, row_in, rpack_out, rpack_in, gpack, grecv, gfin,
    in_sem, v_send, v_recv, u_send, u_recv, g_send, g_recv, r_send, r_recv,
    s1_send, s1_recv, s2_send, s2_recv,
):
    col, gx, gy = lax.axis_index("col"), lax.axis_index("gx"), lax.axis_index("gy")
    group = nx * ny
    me = gx * ny + gy
    cells = planes * rows
    span = cells // CHUNKS
    low, high = col % 2, col // 2
    core = high * 2 + (1 - low)
    chip = (1 - high) * 2 + low
    far = (1 - high) * 2 + (1 - low)

    def exists(dx, dy):
        ok = None
        for d, at, size in ((dx, gx, nx), (dy, gy, ny)):
            if d:
                term = (at + d >= 0) & (at + d < size)
                ok = term if ok is None else ok & term
        return ok

    loads = [
        pltpu.make_async_copy(s, d, in_sem.at[i])
        for i, (s, d) in enumerate(((v_hbm, v_in), (u_hbm, u_in), (w_hbm, w_in)))
    ]
    for load in loads:
        load.start()
    barrier = pltpu.get_barrier_semaphore()

    for other in (core, chip):
        pl.semaphore_signal(barrier, inc=1, device_id={"col": other}, device_id_type=MESH)

    def greet(j, carry):
        @pl.when(j != me)
        def _():
            pl.semaphore_signal(
                barrier, inc=1, device_id={"gx": j // ny, "gy": j % ny}, device_id_type=MESH
            )
        return carry

    lax.fori_loop(0, group, greet, 0)

    for d, (dx, dy) in enumerate(DIRS):
        @pl.when(jnp.logical_not(exists(-dx, -dy)))
        def _():
            for row, corner in ((u_row, pack_in), (row_in, rpack_in)):
                if dy == 0:
                    row[d] = jnp.zeros(row.shape[1:], F32)
                else:
                    corner[d - 2] = jnp.zeros((8, 128), F32)

    lane = lax.broadcasted_iota(jnp.int32, (8, 128), 1)
    loads[0].wait()
    for i in range(cells):
        vx[col, i] = v_in[pl.ds(i, 8, stride=cells), :]
    loads[1].wait()
    for i in range(cells):
        u_own[i // rows, i % rows] = u_in[pl.ds(i, 8, stride=cells), :]
    pack = jnp.zeros((8, 128), F32)
    for z in range(planes):
        for x in range(rows):
            at = z * 8 + x + 1
            tile = u_own[z, x]
            pack = jnp.where(lane == at, pltpu.roll(tile, at + 1, 1), pack)
            pack = jnp.where(lane == at + 64, pltpu.roll(tile, at + 64, 1), pack)
    pack_out[...] = pack

    pl.semaphore_wait(barrier, group + 1)

    def v_copy(slot, sem, target, k):
        part = vx.at[slot, pl.ds(k * span, span)]
        return pltpu.make_async_remote_copy(
            src_ref=part, dst_ref=part, send_sem=v_send.at[sem, k],
            recv_sem=v_recv.at[sem, k], device_id={"col": target}, device_id_type=MESH,
        )

    def u_copy(d):
        dx, dy = DIRS[d]
        if dy == 0:
            src = u_own.at[:, 0 if dx < 0 else rows - 1]
            dst = u_row.at[d]
        else:
            src, dst = pack_out, pack_in.at[d - 2]
        return pltpu.make_async_remote_copy(
            src_ref=src, dst_ref=dst, send_sem=u_send.at[d], recv_sem=u_recv.at[d],
            device_id={"gx": gx + dx, "gy": gy + dy}, device_id_type=MESH,
        )

    def r_copy(d):
        dx, dy = DIRS[d]
        if dy == 0:
            src, dst = local.at[0 if dx < 0 else rows + 1], row_in.at[d]
        else:
            src, dst = rpack_out, rpack_in.at[d - 2]
        return pltpu.make_async_remote_copy(
            src_ref=src, dst_ref=dst, send_sem=r_send.at[d], recv_sem=r_recv.at[d],
            device_id={"gx": gx + dx, "gy": gy + dy}, device_id_type=MESH,
        )

    def each(copies, what, sender):
        for d, (dx, dy) in enumerate(DIRS):
            @pl.when(exists(dx, dy) if sender else exists(-dx, -dy))
            def _():
                getattr(copies(d), what)()

    each(u_copy, "start", True)
    v_chip = [v_copy(col, 0, chip, k) for k in range(CHUNKS)]
    v_core = [v_copy(col, 1, core, k) for k in range(CHUNKS)]
    v_fwd = [v_copy(chip, 2, core, k) for k in range(CHUNKS)]
    for k in range(CHUNKS):
        v_chip[k].start()
        v_core[k].start()

    def hand_on(k):
        v_chip[k].wait_recv()
        v_fwd[k].start()

    loads[2].wait()
    w = w_in[...]
    taps8 = w.shape[0]
    w_hi = w.astype(BF16)
    w_lo = (w - w_hi.astype(F32)).astype(BF16)
    c_at = lax.broadcasted_iota(jnp.int32, (32, 128), 0)
    k_at = lax.broadcasted_iota(jnp.int32, (32, 128), 1)
    same = ((k_at % 64) // 16 == c_at // 8) & (k_at % 8 == c_at % 8)
    pick_hi = jnp.where(same & (k_at < 64), 1.0, 0.0).astype(BF16)
    pick_lo = jnp.where(same & (k_at >= 64), 1.0, 0.0).astype(BF16)
    w_fwd = (
        jnp.dot(w_hi, pick_hi, preferred_element_type=F32)
        + jnp.dot(w_lo, pick_lo, preferred_element_type=F32)
    ).astype(BF16)
    eye_r = lax.broadcasted_iota(jnp.int32, (32, 32), 0)
    eye_c = lax.broadcasted_iota(jnp.int32, (32, 32), 1)
    eye = jnp.where(eye_r == eye_c, 1.0, 0.0).astype(BF16)
    d_r = lax.broadcasted_iota(jnp.int32, (taps8, 2 * taps8), 0)
    d_c = lax.broadcasted_iota(jnp.int32, (taps8, 2 * taps8), 1)
    twice = jnp.where((d_r // 8 == d_c // 16) & (d_r % 8 == d_c % 8), 1.0, 0.0).astype(BF16)
    nt = (((1,), (1,)), ((), ()))
    w_back = []
    for part in (w_hi, w_lo):
        turned = lax.dot_general(eye, part, nt, preferred_element_type=F32).astype(BF16)
        w_back.append(jnp.dot(turned, twice, preferred_element_type=F32))
    w_back = jnp.concatenate(w_back, axis=0).astype(BF16)

    each(u_copy, "wait_recv", False)
    hand_on(0)
    spot = lane % 8
    edge = jnp.zeros((8, 128), F32)
    for first, keep in ((3, lane < 64), (0, lane >= 64)):
        before, mid, after = pack_in[first + 2], pack_in[first + 1], pack_in[first]
        total = jnp.where((spot >= 1) & (spot <= rows), mid, 0.0)
        total = jnp.where(spot == 0, pltpu.roll(before, 128 - rows, 1), total)
        total = jnp.where(spot == rows + 1, pltpu.roll(after, rows, 1), total)
        edge = jnp.where(keep, total, edge)
    zero16 = jnp.zeros((16, 128), BF16)
    for e in range(3):
        for x in range(rows + 2):
            u3[e, 0, x] = zero16
            u3[e, planes + 1, x] = zero16
    for z in range(planes):
        for x in range(rows + 2):
            at = z * 8 + x
            if x == 0:
                tile = u_row[1, z]
            elif x == rows + 1:
                tile = u_row[0, z]
            else:
                tile = u_own[z, x - 1]
            left = jnp.where(
                lane == 127, pltpu.roll(edge, (127 - 64 - at) % 128, 1), pltpu.roll(tile, 127, 1)
            )
            right = jnp.where(
                lane == 0, pltpu.roll(edge, (128 - at) % 128, 1), pltpu.roll(tile, 1, 1)
            )
            u3[0, z + 1, x] = split(left)
            u3[1, z + 1, x] = split(tile)
            u3[2, z + 1, x] = split(right)

    def stack(z):
        return jnp.concatenate(
            [
                jnp.concatenate([u3[e, z + 2 - a, x + 2 - b] for a, b, e in TAPS], axis=0)
                for x in range(rows)
            ],
            axis=1,
        )

    def back(z, carry):
        both = jnp.dot(w_back, stack(z), preferred_element_type=F32)
        for g in range(4):
            for x in range(rows):
                lanes = slice(x * 128, (x + 1) * 128)
                igp[g, z * rows + x] = (
                    both[g * 8 : g * 8 + 8, lanes] + both[32 + g * 8 : 40 + g * 8, lanes]
                )
        return carry

    hand_on(1)
    lax.fori_loop(0, planes // 2, back, 0)
    hand_on(2)
    lax.fori_loop(planes // 2, planes, back, 0)

    def g_copy(slot, to, target):
        return pltpu.make_async_remote_copy(
            src_ref=igp.at[slot], dst_ref=rs.at[to], send_sem=g_send.at[to],
            recv_sem=g_recv.at[to], device_id={"col": target}, device_id_type=MESH,
        )

    g_far, g_core, g_chip = g_copy(far, 1, core), g_copy(core, 0, core), g_copy(chip, 2, chip)
    g_far.start()
    hand_on(3)
    g_core.start()
    g_far.wait_recv()
    for i in range(cells):
        igp[chip, i] = igp[chip, i] + rs[1, i]
    g_chip.start()

    def block(z):
        return jnp.concatenate(
            [
                jnp.concatenate([x2[g, z * rows + x] for g in range(4)], axis=0)
                for x in range(rows)
            ],
            axis=1,
        )

    def weigh(z, total):
        return total + lax.dot_general(block(z), stack(z), nt, preferred_element_type=F32)

    acc[...] = jnp.zeros_like(acc)

    def forward(z, carry):
        cell = block(z)
        y = jnp.dot(w_fwd, jnp.concatenate([cell, cell], axis=0), preferred_element_type=F32)
        for a in range(3):
            for e in range(3):
                for x in range(rows + 2):
                    terms = [
                        y[
                            ((a * 3 + b) * 3 + e) * 8 : ((a * 3 + b) * 3 + e) * 8 + 8,
                            (x + b - 2) * 128 : (x + b - 1) * 128,
                        ]
                        for b in range(3)
                        if 0 <= x + b - 2 < rows
                    ]
                    acc[e, z + 2 - a, x] = functools.reduce(lambda s, t: s + t, terms, acc[e, z + 2 - a, x])
        return carry

    total = jnp.zeros((64, 2 * taps8), F32)
    for k in range(CHUNKS):
        v_core[k].wait_recv()
        for g in (col, chip, core):
            for i in range(k * span, (k + 1) * span):
                x2[g, i] = split(vx[g, i])
        v_fwd[k].wait_recv()
        for i in range(k * span, (k + 1) * span):
            x2[far, i] = split(vx[far, i])
        total = lax.fori_loop(k * planes // CHUNKS, (k + 1) * planes // CHUNKS, weigh, total)
        if k < CHUNKS - 1:
            lax.fori_loop(k * planes // CHUNKS, (k + 1) * planes // CHUNKS, forward, 0)
    folded = jnp.concatenate(
        [total[g * 16 : g * 16 + 8] + total[g * 16 + 8 : g * 16 + 16] for g in range(4)], axis=0
    )
    wide = jnp.concatenate(
        [folded, jnp.zeros((32, 512 - 2 * taps8), F32)], axis=1
    )
    wide = jnp.concatenate([wide, jnp.zeros((96, 512), F32)], axis=0)
    for p in range(PIECES):
        if p % 2 == 0:
            turned = wide[:, (p // 2) * 128 : (p // 2 + 1) * 128].T
        tile = jnp.zeros((8, 128), F32)
        for q in range(4):
            at = (p % 2) * 64 + q * 16
            term = turned[at : at + 8] + turned[at + 8 : at + 16]
            tile = tile + (pltpu.roll(term, q * 32, 1) if q else term)
        gpack[p] = tile

    def s1_copy(i):
        return pltpu.make_async_remote_copy(
            src_ref=gpack.at[i], dst_ref=grecv.at[me], send_sem=s1_send.at[i],
            recv_sem=s1_recv.at[me], device_id={"gx": i // ny, "gy": i % ny}, device_id_type=MESH,
        )

    for i in range(PIECES):
        @pl.when(me != i)
        def _():
            s1_copy(i).start()

    lax.fori_loop(planes - planes // CHUNKS, planes, forward, 0)
    pack = jnp.zeros((8, 128), F32)
    for z in range(planes):
        for x in range(rows + 2):
            at = z * 8 + x
            up, down = acc[0, z + 1, x], acc[2, z + 1, x]
            pack = jnp.where(lane == at, pltpu.roll(up, at + 1, 1), pack)
            pack = jnp.where(lane == at + 64, pltpu.roll(down, at + 64, 1), pack)
            local[x, z] = (
                acc[1, z + 1, x]
                + jnp.where(lane == 0, 0.0, pltpu.roll(up, 1, 1))
                + jnp.where(lane == 127, 0.0, pltpu.roll(down, 127, 1))
            )
    rpack_out[...] = pack
    each(r_copy, "start", True)

    def s2_copy(i, j):
        return pltpu.make_async_remote_copy(
            src_ref=gfin.at[i], dst_ref=gfin.at[i], send_sem=s2_send.at[j],
            recv_sem=s2_recv.at[i], device_id={"gx": j // ny, "gy": j % ny}, device_id_type=MESH,
        )

    def s1_arrival(j):
        return pltpu.make_async_remote_copy(
            src_ref=gpack.at[0], dst_ref=grecv.at[j], send_sem=s1_send.at[0],
            recv_sem=s1_recv.at[j], device_id={"gx": j // ny, "gy": j % ny}, device_id_type=MESH,
        )

    @pl.when(me < PIECES)
    def _():
        grecv[me] = gpack[me]

        def collect(j, total):
            @pl.when(j != me)
            def _():
                s1_arrival(j).wait_recv()
            return total + grecv[j]

        gfin[me] = lax.fori_loop(0, group, collect, jnp.zeros((8, 128), F32)) * scale

        def hand_out(j, carry):
            @pl.when(j != me)
            def _():
                s2_copy(me, j).start()
            return carry

        lax.fori_loop(0, group, hand_out, 0)

    g_core.wait_recv()
    g_chip.wait_recv()
    for i in range(cells):
        grad_ref[pl.ds(i, 8, stride=cells), :] = igp[col, i] + rs[0, i] + rs[2, i]

    each(r_copy, "wait_recv", False)
    edge = jnp.zeros((8, 128), F32)
    for first, keep in ((3, lane < 64), (0, lane >= 64)):
        before, mid, after = rpack_in[first + 2], rpack_in[first + 1], rpack_in[first]
        total = mid + jnp.where(spot == 1, pltpu.roll(before, 128 - rows, 1), 0.0)
        total = total + jnp.where(spot == rows, pltpu.roll(after, rows, 1), 0.0)
        edge = jnp.where(keep, total, edge)
    for z in range(planes):
        for x in range(rows):
            at = z * 8 + x + 1
            tile = local[x + 1, z]
            if x == 0:
                tile = tile + row_in[1, z]
            if x == rows - 1:
                tile = tile + row_in[0, z]
            tile = tile + jnp.where(lane == 0, pltpu.roll(edge, 128 - at, 1), 0.0)
            tile = tile + jnp.where(lane == 127, pltpu.roll(edge, (127 - 64 - at) % 128, 1), 0.0)
            resp_ref[pl.ds(z * rows + x, 8, stride=cells), :] = tile

    for i in range(PIECES):
        @pl.when(me != i)
        def _():
            s2_copy(i, i).wait_recv()
        for q in range(4):
            if i * 4 + q < 27:
                tile = gfin[i]
                if q:
                    tile = pltpu.roll(tile, 128 - q * 32, 1)
                fg_ref[(i * 4 + q) * 8 : (i * 4 + q) * 8 + 8, :] = tile[:, :32]

    each(u_copy, "wait_send", True)
    each(r_copy, "wait_send", True)
    for copy in (*v_chip, *v_core, *v_fwd, g_far, g_core, g_chip):
        copy.wait_send()
    for i in range(PIECES):
        @pl.when(me != i)
        def _():
            s1_copy(i).wait_send()

    @pl.when(me < PIECES)
    def _():
        def left(j, carry):
            @pl.when(j != me)
            def _():
                s2_copy(me, j).wait_send()
            return carry

        lax.fori_loop(0, group, left, 0)


def solution(mesh):
    nx, ny = mesh.shape["gx"], mesh.shape["gy"]

    def shards(volume, filters, upstream):
        own, planes, rows, width = volume.shape
        cells = planes * rows
        scale = (planes * rows * nx * width * ny) ** (-0.5)
        weights = filters.transpose(2, 3, 4, 0, 1).reshape(27 * own, 32)
        tile = (8, 128)
        resp, grad, fg = pl.pallas_call(
            functools.partial(kernel, nx, ny, planes, rows, scale),
            out_shape=(
                jax.ShapeDtypeStruct((own * cells, width), F32),
                jax.ShapeDtypeStruct((own * cells, width), F32),
                jax.ShapeDtypeStruct((27 * own, 32), F32),
            ),
            in_specs=[pl.BlockSpec(memory_space=pl.ANY)] * 3,
            out_specs=(pl.BlockSpec(memory_space=pltpu.VMEM),) * 3,
            scratch_shapes=[
                pltpu.VMEM((own * cells, width), F32),
                pltpu.VMEM((27 * own, 32), F32),
                pltpu.VMEM((own * cells, width), F32),
                pltpu.VMEM((4, cells) + tile, F32),
                pltpu.VMEM((4, cells, 16, 128), BF16),
                pltpu.VMEM((planes, rows) + tile, F32),
                pltpu.VMEM((2, planes) + tile, F32),
                pltpu.VMEM(tile, F32),
                pltpu.VMEM((6,) + tile, F32),
                pltpu.VMEM((3, planes + 2, rows + 2, 16, 128), BF16),
                pltpu.VMEM((4, cells) + tile, F32),
                pltpu.VMEM((3, cells) + tile, F32),
                pltpu.VMEM((3, planes + 2, rows + 2) + tile, F32),
                pltpu.VMEM((rows + 2, planes) + tile, F32),
                pltpu.VMEM((2, planes) + tile, F32),
                pltpu.VMEM(tile, F32),
                pltpu.VMEM((6,) + tile, F32),
                pltpu.VMEM((PIECES,) + tile, F32),
                pltpu.VMEM((nx * ny,) + tile, F32),
                pltpu.VMEM((PIECES,) + tile, F32),
                pltpu.SemaphoreType.DMA((3,)),
                pltpu.SemaphoreType.DMA((3, CHUNKS)),
                pltpu.SemaphoreType.DMA((3, CHUNKS)),
                pltpu.SemaphoreType.DMA((8,)),
                pltpu.SemaphoreType.DMA((8,)),
                pltpu.SemaphoreType.DMA((3,)),
                pltpu.SemaphoreType.DMA((3,)),
                pltpu.SemaphoreType.DMA((8,)),
                pltpu.SemaphoreType.DMA((8,)),
                pltpu.SemaphoreType.DMA((PIECES,)),
                pltpu.SemaphoreType.DMA((nx * ny,)),
                pltpu.SemaphoreType.DMA((nx * ny,)),
                pltpu.SemaphoreType.DMA((PIECES,)),
            ],
            compiler_params=pltpu.CompilerParams(
                collective_id=0, has_side_effects=True, vmem_limit_bytes=63 * 1024 * 1024
            ),
        )(
            volume.reshape(own * cells, width),
            weights,
            upstream.reshape(own * cells, width),
        )
        return (
            resp.reshape(volume.shape),
            grad.reshape(volume.shape),
            fg.reshape(3, 3, 3, own, 32).transpose(3, 4, 0, 1, 2),
        )

    return jax.shard_map(
        shards,
        mesh=mesh,
        in_specs=(
            P("col", None, "gx", "gy"),
            P("col", None, None, None, None),
            P("col", None, "gx", "gy"),
        ),
        out_specs=(
            P("col", None, "gx", "gy"),
            P("col", None, "gx", "gy"),
            P("col", None, None, None, None),
        ),
        check_vma=False,
    )
```
